32 devices in a mesh: row: 16 (over z, x, core), col: 2 (over y).
Axes of the slice: x: 2, y: 2, z: 4, core: 2. Of those that a mesh axis runs over, the one named last changes fastest.
Arguments:
- amplitudes: float32 [2, 16, 2, 262144], P(None, 'row', 'col'), may hold values from -6 to 6
- gate_matrices: float32 [5, 4, 2, 128, 128], replicated, may hold values from -0.375 to 0.375
- permutation: int32 [16], replicated, may hold values from 0 to 15, each once
Outputs:
- evolved: float32 [2, 16, 2, 262144], P(None, 'row', 'col')
The draws below stay inside these ranges and needn't reach their ends.
Inputs may be any that keep to these rules, and one draw needn't show every extreme that they name: `permutation`: each value from 0 to 15 appears once.
All inputs are finite; a program needn't handle non-finite values.
Results may differ from the reference program's by a relative error of at most 0.00014.
Values sent between devices are 32-bit elements; how exact they have to be, the bound alone decides.
A program may use at most 64 MiB of HBM per device.

```python
import jax
import jax.numpy as jnp
from jax import lax

GD = 128
AMP_DEV = 262144
SEGS = 5
GATES = 4
N_ROW = 16
N_COL = 2


def shard_levels(own_key, shape, shards, smallest, top_value):
    level = 1.0
    for position, shards_of in shards:
        heights = jax.random.uniform(jax.random.fold_in(jax.random.fold_in(own_key, 6), position), (shards_of,), jnp.float32, smallest / len(shards), top_value / len(shards))
        level = level * jnp.repeat(jnp.exp(heights), shape[position] // shards_of).reshape((-1,) + (1,) * (len(shape) - 1 - position))
    return level


def noise(key, shape, scale, bound, cuts=(), dtype=jnp.bfloat16):
    values = scale * jax.random.normal(key, shape, jnp.float32)
    if cuts:
        values = values * shard_levels(key, shape, cuts, -0.22, 0.18)
    return jnp.clip(values, -bound, bound).astype(dtype)


def setup_inputs(seed: int = 0) -> dict:
    keys = jax.random.split(jax.random.key(seed), 4)
    return {
        "amplitudes": noise(keys[0], (2, N_ROW, N_COL, AMP_DEV), 1.0, 6.0, ((1, 16), (2, 2)), jnp.float32),
        "gate_matrices": noise(keys[1], (SEGS, GATES, 2, GD, GD), (2 * GD) ** -0.5, 0.375, (), jnp.float32),
        "permutation": jax.random.permutation(keys[2], N_ROW).astype(jnp.int32),
    }


HIGHEST = lax.Precision.HIGHEST
GATE_KINDS = ("top", "mid", "low", "top")


def stacked(gate_mat):
    real_part = gate_mat[0]
    imag_part = gate_mat[1]
    top_rows = jnp.concatenate([real_part, -imag_part], axis=1)
    bottom_rows = jnp.concatenate([imag_part, real_part], axis=1)
    return jnp.concatenate([top_rows, bottom_rows], axis=0)


def gate_whole(field, gate_mat, kind):
    gate_size = gate_mat.shape[-1]
    real_quad = stacked(gate_mat).reshape(2, gate_size, 2, gate_size)
    groups = field.shape[1]
    amp_count = field.shape[2]
    if kind == "top":
        shaped = field.reshape(2, groups, gate_size, amp_count // gate_size)
        result = jnp.einsum("djck,cpkm->dpjm", real_quad, shaped, precision=HIGHEST)
    elif kind == "mid":
        shaped = field.reshape(2, groups, amp_count // (gate_size * gate_size), gate_size, gate_size)
        result = jnp.einsum("djck,cpakb->dpajb", real_quad, shaped, precision=HIGHEST)
    else:
        shaped = field.reshape(2, groups, amp_count // gate_size, gate_size)
        result = jnp.einsum("djck,cpmk->dpmj", real_quad, shaped, precision=HIGHEST)
    return result.reshape(2, groups, amp_count)


def segment(field, seg_mats):
    full_shape = field.shape
    flat_field = field.reshape(2, N_ROW * N_COL, AMP_DEV)
    for number in range(seg_mats.shape[0]):
        flat_field = gate_whole(flat_field, seg_mats[number], GATE_KINDS[number])
    return flat_field.reshape(full_shape)


def swap_row_bit(field, bit_pos):
    stride = 2 ** bit_pos
    shaped = field.reshape(2, N_ROW // (2 * stride), 2, stride, N_COL, 2, AMP_DEV // 2)
    return jnp.swapaxes(shaped, 2, 5).reshape(2, N_ROW, N_COL, AMP_DEV)


def swap_col_top(field):
    shaped = field.reshape(2, N_ROW, 2, N_COL // 2, 2, AMP_DEV // 2)
    return jnp.swapaxes(shaped, 2, 4).reshape(2, N_ROW, N_COL, AMP_DEV)


def reference(amplitudes, gate_matrices, permutation):
    row_bits = int(N_ROW).bit_length() - 1
    field = segment(amplitudes, gate_matrices[0])
    field = swap_row_bit(field, 0)
    field = segment(field, gate_matrices[1])
    field = swap_row_bit(field, row_bits - 1)
    field = segment(field, gate_matrices[2])
    shaped = field.reshape(2, N_ROW, N_COL, N_ROW, AMP_DEV // N_ROW)
    shaped = jnp.swapaxes(shaped, 1, 3)
    shaped = shaped[:, :, :, permutation, :]
    field = shaped.reshape(2, N_ROW, N_COL, AMP_DEV)
    field = segment(field, gate_matrices[3])
    field = swap_col_top(field)
    return segment(field, gate_matrices[4])
```

```python
import functools

import jax
import jax.numpy as jnp
from jax import lax
from jax.experimental import pallas as pl
from jax.experimental.pallas import tpu as pltpu
from jax.sharding import PartitionSpec as P

HIGHEST = lax.Precision.HIGHEST
MESH = pl.DeviceIdType.MESH
F32 = jnp.float32
BF16 = jnp.bfloat16


def split(value):
    high = value.astype(BF16)
    return high, (value - high.astype(F32)).astype(BF16)


def dot32(left, right):
    return jnp.dot(left, right, preferred_element_type=F32)


def product(left, right):
    left_high, left_low = split(left)
    right_high, right_low = split(right)
    return (
        dot32(left_high, right_high)
        + dot32(left_high, right_low)
        + dot32(left_low, right_high)
    )


def real_form(real_part, imag_part):
    return jnp.concatenate(
        [
            jnp.concatenate([real_part, -imag_part], axis=1),
            jnp.concatenate([imag_part, real_part], axis=1),
        ],
        axis=0,
    )


def real_form_transposed(real_part, imag_part):
    real_t, imag_t = real_part.T, imag_part.T
    return jnp.concatenate(
        [
            jnp.concatenate([real_t, imag_t], axis=1),
            jnp.concatenate([-imag_t, real_t], axis=1),
        ],
        axis=0,
    )


def kernel(
    rows,
    cols,
    amp_ref,
    gates_ref,
    mids_ref,
    first_ref,
    out_ref,
    state,
    weight,
    low_weight,
    arrived,
    stage,
    blocks,
    swap_send,
    swap_recv,
    map_send,
    map_recv,
):
    kk, _, high, low, lanes = state.shape
    order = high * low
    chunks = kk // 2
    rest = order // rows
    half = high // 2
    r = lax.axis_index("row")
    c = lax.axis_index("col")

    barrier = pltpu.get_barrier_semaphore()
    near = r + 1 - 2 * (r % 2)
    far_bit = r // (rows // 2)
    far = r + rows // 2 - rows * far_bit
    col_bit = c // (cols // 2)
    across = c + cols // 2 - cols * col_bit
    for step in range(1, rows):
        pl.semaphore_signal(
            barrier, inc=1, device_id=((r + step) % rows, c), device_id_type=MESH
        )
    pl.semaphore_signal(barrier, inc=1, device_id=(r, across), device_id_type=MESH)

    def set_weight(real_part, imag_part):
        top, bottom = split(real_form(real_part, imag_part))
        size = 2 * order
        weight[:, 0:size] = top
        weight[:, size : 2 * size] = top
        weight[:, 2 * size : 3 * size] = bottom

    def apply(value):
        top, bottom = split(value)
        return dot32(weight[...], jnp.concatenate([top, bottom, top], axis=0))

    def put(i, result):
        state[2 * i] = result[:, :lanes].reshape(2, high, low, lanes)
        state[2 * i + 1] = result[:, lanes:].reshape(2, high, low, lanes)

    def get(i):
        return jnp.concatenate(
            [
                state[2 * i].reshape(2 * order, lanes),
                state[2 * i + 1].reshape(2 * order, lanes),
            ],
            axis=1,
        )

    def top_step(i):
        put(i, apply(get(i)))

    def middle(seg):
        set_weight(mids_ref[seg, 0], mids_ref[seg, 1])

        def step(p, carry):
            def part(position):
                return jnp.concatenate(
                    [
                        state[:, 0, position].reshape(order, lanes),
                        state[:, 1, position].reshape(order, lanes),
                    ],
                    axis=0,
                )

            result = apply(jnp.concatenate([part(2 * p), part(2 * p + 1)], axis=1))
            for own in range(2):
                piece = result[:, own * lanes : (own + 1) * lanes]
                for d in range(2):
                    state[:, d, 2 * p + own] = piece[
                        d * order : (d + 1) * order
                    ].reshape(kk, low, lanes)
            return carry

        lax.fori_loop(0, high // 2, step, 0)

    def swap_copy(which, i, bit, device):
        return pltpu.make_async_remote_copy(
            src_ref=state.at[pl.ds(2 * i, 2), :, pl.ds((1 - bit) * half, half)],
            dst_ref=arrived.at[which, pl.ds(2 * i, 2)],
            send_sem=swap_send.at[which, i],
            recv_sem=swap_recv.at[which, i],
            device_id=device,
            device_id_type=MESH,
        )

    def lows(value):
        parts = jnp.concatenate([value[0], value[1]], axis=1)
        top, bottom = split(parts)
        joined = jnp.concatenate([top, bottom, top], axis=1)
        result = dot32(joined, low_weight[...])
        return jnp.stack([result[:, :lanes], result[:, lanes:]], axis=0)

    def swap_out(seg, which, bit, device):
        set_weight(gates_ref[seg, 3, 0], gates_ref[seg, 3, 1])

        def send(i, carry):
            top_step(i)
            swap_copy(which, i, bit, device).start()
            return carry

        lax.fori_loop(0, chunks, send, 0)

    def swap_in(seg, which, bit, device, with_lows):
        set_weight(gates_ref[seg, 0, 0], gates_ref[seg, 0, 1])

        def receive(i, carry):
            swap_copy(which, i, bit, device).wait()
            for own in range(2):
                piece = arrived[which, 2 * i + own]
                if with_lows:
                    piece = lows(piece.reshape(2, half * low, lanes)).reshape(
                        piece.shape
                    )
                state[2 * i + own, :, pl.ds((1 - bit) * half, half)] = piece
            top_step(i)
            return carry

        lax.fori_loop(0, chunks, receive, 0)

    set_weight(gates_ref[0, 0, 0], gates_ref[0, 0, 1])

    def load(i, carry):
        value = jnp.concatenate(
            [
                amp_ref[pl.ds(2 * i, 2 * order, stride=kk), :],
                amp_ref[pl.ds(2 * i + 1, 2 * order, stride=kk), :],
            ],
            axis=1,
        )
        put(i, apply(value))
        return carry

    lax.fori_loop(0, chunks, load, 0)
    middle(0)
    pl.semaphore_wait(barrier, rows)
    near_bit = r % 2
    swap_out(0, 0, near_bit, (near, c))
    swap_in(1, 0, near_bit, (near, c), False)
    middle(1)
    swap_out(1, 1, far_bit, (far, c))

    merged = real_form_transposed(gates_ref[0, 2, 0], gates_ref[0, 2, 1])
    for seg in range(1, gates_ref.shape[0]):
        merged = product(
            merged, real_form_transposed(gates_ref[seg, 2, 0], gates_ref[seg, 2, 1])
        )
    top, bottom = split(merged)
    low_weight[0 : 2 * lanes] = top
    low_weight[2 * lanes : 4 * lanes] = top
    low_weight[4 * lanes : 6 * lanes] = bottom

    def keep(i, carry):
        piece = state[i, :, pl.ds(far_bit * half, half)]
        state[i, :, pl.ds(far_bit * half, half)] = lows(
            piece.reshape(2, half * low, lanes)
        ).reshape(piece.shape)
        return carry

    lax.fori_loop(0, kk, keep, 0)
    swap_in(2, 1, far_bit, (far, c), True)
    middle(2)
    set_weight(gates_ref[2, 3, 0], gates_ref[2, 3, 1])

    def map_copy(i, step):
        target = (r + step) % rows
        return pltpu.make_async_remote_copy(
            src_ref=stage.at[i, target],
            dst_ref=blocks.at[i, r],
            send_sem=map_send.at[i, step],
            recv_sem=map_recv.at[i, step],
            device_id=(target, c),
            device_id_type=MESH,
        )

    def map_out(i, carry):
        result = apply(get(i))
        for own in range(2):
            for d in range(2):
                piece = result[
                    d * order : (d + 1) * order, own * lanes : (own + 1) * lanes
                ]
                if rest == 8:
                    stage[i, :, d, own * rest : (own + 1) * rest] = piece.reshape(
                        rows, rest, lanes
                    )
                else:
                    for t in range(rows):
                        stage[i, t, d, own * rest : (own + 1) * rest] = piece[
                            t * rest : (t + 1) * rest
                        ]
        for step in range(1, rows):
            map_copy(i, step).start()
        blocks[i, r] = stage[i, r]
        return carry

    lax.fori_loop(0, chunks, map_out, 0)
    set_weight(first_ref[0], first_ref[1])

    def map_in(i, carry):
        for step in range(1, rows):
            map_copy(i, step).wait()
        columns = []
        for own in range(2):
            if rest == 8:
                pieces = [
                    blocks[i, :, d, own * rest : (own + 1) * rest].reshape(order, lanes)
                    for d in range(2)
                ]
            else:
                pieces = [
                    blocks[i, s, d, own * rest : (own + 1) * rest]
                    for d in range(2)
                    for s in range(rows)
                ]
            columns.append(jnp.concatenate(pieces, axis=0))
        put(i, apply(jnp.concatenate(columns, axis=1)))
        return carry

    lax.fori_loop(0, chunks, map_in, 0)
    middle(3)
    swap_out(3, 2, col_bit, (r, across))
    swap_in(4, 2, col_bit, (r, across), False)
    middle(4)
    set_weight(gates_ref[4, 3, 0], gates_ref[4, 3, 1])

    def finish(i, carry):
        result = apply(get(i))
        out_ref[pl.ds(2 * i, 2 * order, stride=kk), :] = result[:, :lanes]
        out_ref[pl.ds(2 * i + 1, 2 * order, stride=kk), :] = result[:, lanes:]
        return carry

    lax.fori_loop(0, chunks, finish, 0)


def body(amplitudes, gate_matrices, permutation):
    rows = lax.axis_size("row")
    cols = lax.axis_size("col")
    segs = gate_matrices.shape[0]
    order = gate_matrices.shape[-1]
    amp_count = amplitudes.shape[-1]
    high = amp_count // (order * order)
    low = order // high
    kk = order // low
    rest = order // rows
    chunks = kk // 2
    mids = gate_matrices[:, 1].reshape(segs, 2, low, kk, low, kk)
    mids = mids.transpose(0, 1, 3, 2, 5, 4).reshape(segs, 2, order, order)
    chosen = (permutation[:, None] == jnp.arange(rows)[None, :]).astype(F32)
    first = jnp.einsum(
        "xjtw,ts->xjsw",
        gate_matrices[3, 0].reshape(2, order, rows, rest),
        chosen,
        precision=HIGHEST,
    ).reshape(2, order, order)
    vmem = pl.BlockSpec(memory_space=pltpu.VMEM)
    result = pl.pallas_call(
        functools.partial(kernel, rows, cols),
        out_shape=jax.ShapeDtypeStruct((2 * amp_count // order, order), F32),
        in_specs=[vmem] * 4,
        out_specs=vmem,
        scratch_shapes=[
            pltpu.VMEM((kk, 2, high, low, order), F32),
            pltpu.VMEM((2 * order, 6 * order), BF16),
            pltpu.VMEM((6 * order, 2 * order), BF16),
            pltpu.VMEM((3, kk, 2, high // 2, low, order), F32),
            pltpu.VMEM((chunks, rows, 2, 2 * rest, order), F32),
            pltpu.VMEM((chunks, rows, 2, 2 * rest, order), F32),
            pltpu.SemaphoreType.DMA((3, chunks)),
            pltpu.SemaphoreType.DMA((3, chunks)),
            pltpu.SemaphoreType.DMA((chunks, rows)),
            pltpu.SemaphoreType.DMA((chunks, rows)),
        ],
        compiler_params=pltpu.CompilerParams(
            collective_id=0, has_side_effects=True, vmem_limit_bytes=40 * 2**20
        ),
    )(amplitudes.reshape(2 * amp_count // order, order), gate_matrices, mids, first)
    return result.reshape(amplitudes.shape)


def solution(mesh):
    placed = (P(None, "row", "col", None), P(), P())
    return jax.shard_map(
        body, mesh=mesh, in_specs=placed, out_specs=P(None, "row", "col", None), check_vma=False
    )
```

```python
import functools

import jax
import jax.numpy as jnp
from jax import lax
from jax.experimental import pallas as pl
from jax.experimental.pallas import tpu as pltpu
from jax.sharding import PartitionSpec as P

HIGHEST = lax.Precision.HIGHEST
MESH = pl.DeviceIdType.MESH
F32 = jnp.float32
BF16 = jnp.bfloat16


def split(value):
    high = value.astype(BF16)
    return high, (value - high.astype(F32)).astype(BF16)


def dot32(left, right):
    return jnp.dot(left, right, preferred_element_type=F32)


def product(left, right):
    left_high, left_low = split(left)
    right_high, right_low = split(right)
    return (
        dot32(left_high, right_high)
        + dot32(left_high, right_low)
        + dot32(left_low, right_high)
    )


def real_form(real_part, imag_part):
    return jnp.concatenate(
        [
            jnp.concatenate([real_part, -imag_part], axis=1),
            jnp.concatenate([imag_part, real_part], axis=1),
        ],
        axis=0,
    )


def real_form_transposed(real_part, imag_part):
    real_t, imag_t = real_part.T, imag_part.T
    return jnp.concatenate(
        [
            jnp.concatenate([real_t, imag_t], axis=1),
            jnp.concatenate([-imag_t, real_t], axis=1),
        ],
        axis=0,
    )


def kernel(
    rows,
    cols,
    amp_ref,
    gates_ref,
    first_ref,
    out_ref,
    state,
    weight,
    low_weight,
    arrived,
    stage,
    blocks,
    swap_send,
    swap_recv,
    map_send,
    map_recv,
):
    kk, _, high, low, lanes = state.shape
    order = high * low
    chunks = kk // 2
    rest = order // rows
    half = high // 2
    r = lax.axis_index("row")
    c = lax.axis_index("col")

    barrier = pltpu.get_barrier_semaphore()
    near = r + 1 - 2 * (r % 2)
    far_bit = r // (rows // 2)
    far = r + rows // 2 - rows * far_bit
    col_bit = c // (cols // 2)
    across = c + cols // 2 - cols * col_bit
    for step in range(1, rows):
        pl.semaphore_signal(
            barrier, inc=1, device_id=((r + step) % rows, c), device_id_type=MESH
        )
    pl.semaphore_signal(barrier, inc=1, device_id=(r, across), device_id_type=MESH)

    def place_weight(top, bottom):
        size = 2 * order
        weight[:, 0:size] = top
        weight[:, size : 2 * size] = top
        weight[:, 2 * size : 3 * size] = bottom

    def set_weight(real_part, imag_part):
        place_weight(*split(real_form(real_part, imag_part)))

    def reorder_matrix():
        new = lax.broadcasted_iota(jnp.int32, (order, order), 0)
        old = lax.broadcasted_iota(jnp.int32, (order, order), 1)
        return ((new % low) * kk + new // low == old).astype(F32).astype(BF16)

    def apply(value):
        top, bottom = split(value)
        return dot32(weight[...], jnp.concatenate([top, bottom, top], axis=0))

    def put(i, result):
        state[2 * i] = result[:, :lanes].reshape(2, high, low, lanes)
        state[2 * i + 1] = result[:, lanes:].reshape(2, high, low, lanes)

    def get(i):
        return jnp.concatenate(
            [
                state[2 * i].reshape(2 * order, lanes),
                state[2 * i + 1].reshape(2 * order, lanes),
            ],
            axis=1,
        )

    def top_step(i):
        put(i, apply(get(i)))

    def middle(seg):
        reorder = reorder_matrix()

        def moved(part):
            rows_moved = dot32(reorder, part).astype(BF16)
            return lax.dot_general(
                rows_moved, reorder, (((1,), (1,)), ((), ())), preferred_element_type=F32
            ).astype(BF16)

        real_parts = split(gates_ref[seg, 1, 0])
        imag_parts = split(gates_ref[seg, 1, 1])
        place_weight(
            *(real_form(moved(re), moved(im)) for re, im in zip(real_parts, imag_parts))
        )

        def step(p, carry):
            def part(position):
                return jnp.concatenate(
                    [
                        state[:, 0, position].reshape(order, lanes),
                        state[:, 1, position].reshape(order, lanes),
                    ],
                    axis=0,
                )

            result = apply(jnp.concatenate([part(2 * p), part(2 * p + 1)], axis=1))
            for own in range(2):
                piece = result[:, own * lanes : (own + 1) * lanes]
                for d in range(2):
                    state[:, d, 2 * p + own] = piece[
                        d * order : (d + 1) * order
                    ].reshape(kk, low, lanes)
            return carry

        lax.fori_loop(0, high // 2, step, 0)

    def swap_copy(which, i, bit, device):
        return pltpu.make_async_remote_copy(
            src_ref=state.at[pl.ds(2 * i, 2), :, pl.ds((1 - bit) * half, half)],
            dst_ref=arrived.at[which, pl.ds(2 * i, 2)],
            send_sem=swap_send.at[which, i],
            recv_sem=swap_recv.at[which, i],
            device_id=device,
            device_id_type=MESH,
        )

    def lows(value):
        parts = jnp.concatenate([value[0], value[1]], axis=1)
        top, bottom = split(parts)
        joined = jnp.concatenate([top, bottom, top], axis=1)
        result = dot32(joined, low_weight[...])
        return jnp.stack([result[:, :lanes], result[:, lanes:]], axis=0)

    def swap_out(seg, which, bit, device):
        set_weight(gates_ref[seg, 3, 0], gates_ref[seg, 3, 1])

        def send(i, carry):
            top_step(i)
            swap_copy(which, i, bit, device).start()
            return carry

        lax.fori_loop(0, chunks, send, 0)

    def swap_in(seg, which, bit, device, with_lows):
        set_weight(gates_ref[seg, 0, 0], gates_ref[seg, 0, 1])

        def receive(i, carry):
            swap_copy(which, i, bit, device).wait()
            for own in range(2):
                piece = arrived[which, 2 * i + own]
                if with_lows:
                    piece = lows(piece.reshape(2, half * low, lanes)).reshape(
                        piece.shape
                    )
                state[2 * i + own, :, pl.ds((1 - bit) * half, half)] = piece
            top_step(i)
            return carry

        lax.fori_loop(0, chunks, receive, 0)

    set_weight(gates_ref[0, 0, 0], gates_ref[0, 0, 1])

    def load(i, carry):
        value = jnp.concatenate(
            [
                amp_ref[pl.ds(2 * i, 2 * order, stride=kk), :],
                amp_ref[pl.ds(2 * i + 1, 2 * order, stride=kk), :],
            ],
            axis=1,
        )
        put(i, apply(value))
        return carry

    lax.fori_loop(0, chunks, load, 0)
    middle(0)
    pl.semaphore_wait(barrier, rows)
    near_bit = r % 2
    swap_out(0, 0, near_bit, (near, c))
    swap_in(1, 0, near_bit, (near, c), False)
    middle(1)
    swap_out(1, 1, far_bit, (far, c))

    merged = real_form_transposed(gates_ref[0, 2, 0], gates_ref[0, 2, 1])
    for seg in range(1, gates_ref.shape[0]):
        merged = product(
            merged, real_form_transposed(gates_ref[seg, 2, 0], gates_ref[seg, 2, 1])
        )
    top, bottom = split(merged)
    low_weight[0 : 2 * lanes] = top
    low_weight[2 * lanes : 4 * lanes] = top
    low_weight[4 * lanes : 6 * lanes] = bottom

    def keep(i, carry):
        piece = state[i, :, pl.ds(far_bit * half, half)]
        state[i, :, pl.ds(far_bit * half, half)] = lows(
            piece.reshape(2, half * low, lanes)
        ).reshape(piece.shape)
        return carry

    lax.fori_loop(0, kk, keep, 0)
    swap_in(2, 1, far_bit, (far, c), True)
    middle(2)
    set_weight(gates_ref[2, 3, 0], gates_ref[2, 3, 1])

    def map_copy(i, step):
        target = (r + step) % rows
        return pltpu.make_async_remote_copy(
            src_ref=stage.at[i, target],
            dst_ref=blocks.at[i, r],
            send_sem=map_send.at[i, step],
            recv_sem=map_recv.at[i, step],
            device_id=(target, c),
            device_id_type=MESH,
        )

    def map_out(i, carry):
        result = apply(get(i))
        for own in range(2):
            for d in range(2):
                piece = result[
                    d * order : (d + 1) * order, own * lanes : (own + 1) * lanes
                ]
                if rest == 8:
                    stage[i, :, d, own * rest : (own + 1) * rest] = piece.reshape(
                        rows, rest, lanes
                    )
                else:
                    for t in range(rows):
                        stage[i, t, d, own * rest : (own + 1) * rest] = piece[
                            t * rest : (t + 1) * rest
                        ]
        for step in range(1, rows):
            map_copy(i, step).start()
        blocks[i, r] = stage[i, r]
        return carry

    lax.fori_loop(0, chunks, map_out, 0)
    set_weight(first_ref[0], first_ref[1])

    def map_in(i, carry):
        for step in range(1, rows):
            map_copy(i, step).wait()
        columns = []
        for own in range(2):
            if rest == 8:
                pieces = [
                    blocks[i, :, d, own * rest : (own + 1) * rest].reshape(order, lanes)
                    for d in range(2)
                ]
            else:
                pieces = [
                    blocks[i, s, d, own * rest : (own + 1) * rest]
                    for d in range(2)
                    for s in range(rows)
                ]
            columns.append(jnp.concatenate(pieces, axis=0))
        put(i, apply(jnp.concatenate(columns, axis=1)))
        return carry

    lax.fori_loop(0, chunks, map_in, 0)
    middle(3)
    swap_out(3, 2, col_bit, (r, across))
    swap_in(4, 2, col_bit, (r, across), False)
    middle(4)
    set_weight(gates_ref[4, 3, 0], gates_ref[4, 3, 1])

    def finish(i, carry):
        result = apply(get(i))
        out_ref[pl.ds(2 * i, 2 * order, stride=kk), :] = result[:, :lanes]
        out_ref[pl.ds(2 * i + 1, 2 * order, stride=kk), :] = result[:, lanes:]
        return carry

    lax.fori_loop(0, chunks, finish, 0)


def body(amplitudes, gate_matrices, permutation):
    rows = lax.axis_size("row")
    cols = lax.axis_size("col")
    order = gate_matrices.shape[-1]
    amp_count = amplitudes.shape[-1]
    high = amp_count // (order * order)
    low = order // high
    kk = order // low
    rest = order // rows
    chunks = kk // 2
    chosen = (permutation[:, None] == jnp.arange(rows)[None, :]).astype(F32)
    first = jnp.einsum(
        "xjtw,ts->xjsw",
        gate_matrices[3, 0].reshape(2, order, rows, rest),
        chosen,
        precision=HIGHEST,
    ).reshape(2, order, order)
    vmem = pl.BlockSpec(memory_space=pltpu.VMEM)
    result = pl.pallas_call(
        functools.partial(kernel, rows, cols),
        out_shape=jax.ShapeDtypeStruct((2 * amp_count // order, order), F32),
        in_specs=[vmem] * 3,
        out_specs=vmem,
        scratch_shapes=[
            pltpu.VMEM((kk, 2, high, low, order), F32),
            pltpu.VMEM((2 * order, 6 * order), BF16),
            pltpu.VMEM((6 * order, 2 * order), BF16),
            pltpu.VMEM((3, kk, 2, high // 2, low, order), F32),
            pltpu.VMEM((chunks, rows, 2, 2 * rest, order), F32),
            pltpu.VMEM((chunks, rows, 2, 2 * rest, order), F32),
            pltpu.SemaphoreType.DMA((3, chunks)),
            pltpu.SemaphoreType.DMA((3, chunks)),
            pltpu.SemaphoreType.DMA((chunks, rows)),
            pltpu.SemaphoreType.DMA((chunks, rows)),
        ],
        compiler_params=pltpu.CompilerParams(
            collective_id=0, has_side_effects=True, vmem_limit_bytes=40 * 2**20
        ),
    )(amplitudes.reshape(2 * amp_count // order, order), gate_matrices, first)
    return result.reshape(amplitudes.shape)


def solution(mesh):
    placed = (P(None, "row", "col", None), P(), P())
    return jax.shard_map(
        body, mesh=mesh, in_specs=placed, out_specs=P(None, "row", "col", None), check_vma=False
    )
```

```python
import functools

import jax
import jax.numpy as jnp
from jax import lax
from jax.experimental import pallas as pl
from jax.experimental.pallas import tpu as pltpu
from jax.sharding import PartitionSpec as P

HIGHEST = lax.Precision.HIGHEST
MESH = pl.DeviceIdType.MESH
F32 = jnp.float32
BF16 = jnp.bfloat16


def split(value):
    high = value.astype(BF16)
    return high, (value - high.astype(F32)).astype(BF16)


def dot32(left, right):
    return jnp.dot(left, right, preferred_element_type=F32)


def product(left, right):
    left_high, left_low = split(left)
    right_high, right_low = split(right)
    return (
        dot32(left_high, right_high)
        + dot32(left_high, right_low)
        + dot32(left_low, right_high)
    )


def real_form(real_part, imag_part):
    return jnp.concatenate(
        [
            jnp.concatenate([real_part, -imag_part], axis=1),
            jnp.concatenate([imag_part, real_part], axis=1),
        ],
        axis=0,
    )


def real_form_transposed(real_part, imag_part):
    real_t, imag_t = real_part.T, imag_part.T
    return jnp.concatenate(
        [
            jnp.concatenate([real_t, imag_t], axis=1),
            jnp.concatenate([-imag_t, real_t], axis=1),
        ],
        axis=0,
    )


def kernel(
    rows,
    cols,
    amp_ref,
    gates_ref,
    first_ref,
    out_ref,
    state,
    weight,
    low_weight,
    arrived,
    stage,
    blocks,
    swap_send,
    swap_recv,
    map_send,
    map_recv,
):
    kk, _, high, low, lanes = state.shape
    order = high * low
    chunks = kk // 2
    rest = order // rows
    half = high // 2
    r = lax.axis_index("row")
    c = lax.axis_index("col")

    barrier = pltpu.get_barrier_semaphore()
    near = r + 1 - 2 * (r % 2)
    far_bit = r // (rows // 2)
    far = r + rows // 2 - rows * far_bit
    col_bit = c // (cols // 2)
    across = c + cols // 2 - cols * col_bit
    for step in range(1, rows):
        pl.semaphore_signal(
            barrier, inc=1, device_id=((r + step) % rows, c), device_id_type=MESH
        )
    pl.semaphore_signal(barrier, inc=1, device_id=(r, across), device_id_type=MESH)

    count = chunks // 2
    mid_lane = lanes // 2

    def place_weight(slot, top, bottom):
        size = 2 * order
        weight[slot, :, 0:size] = top
        weight[slot, :, size : 2 * size] = top
        weight[slot, :, 2 * size : 3 * size] = bottom

    def set_top(slot, source):
        place_weight(slot, *split(real_form(source[0], source[1])))

    def reorder_matrix():
        new = lax.broadcasted_iota(jnp.int32, (order, order), 0)
        old = lax.broadcasted_iota(jnp.int32, (order, order), 1)
        outer = new // low
        place = (new % low) * kk + 2 * (outer % chunks) + outer // chunks
        return (place == old).astype(F32).astype(BF16)

    def set_middle(slot, source):
        reorder = reorder_matrix()

        def moved(part):
            rows_moved = dot32(reorder, part).astype(BF16)
            return lax.dot_general(
                rows_moved, reorder, (((1,), (1,)), ((), ())), preferred_element_type=F32
            ).astype(BF16)

        real_parts = split(source[0])
        imag_parts = split(source[1])
        place_weight(
            slot,
            *(real_form(moved(re), moved(im)) for re, im in zip(real_parts, imag_parts)),
        )

    def crossed(first, second):
        return (
            jnp.concatenate([first[:, :mid_lane], second[:, :mid_lane]], axis=1),
            jnp.concatenate([first[:, mid_lane:], second[:, mid_lane:]], axis=1),
        )

    def apply(slot, value):
        top, bottom = split(value)
        return dot32(weight[slot], jnp.concatenate([top, bottom, top], axis=0))

    def put(i, result):
        state[2 * i] = result[:, :lanes].reshape(2, high, low, lanes)
        state[2 * i + 1] = result[:, lanes:].reshape(2, high, low, lanes)

    def get(i):
        return jnp.concatenate(
            [
                state[2 * i].reshape(2 * order, lanes),
                state[2 * i + 1].reshape(2 * order, lanes),
            ],
            axis=1,
        )

    def top_step(slot, i):
        put(i, apply(slot, get(i)))

    def each(h, step):
        def run(i, carry):
            step(i)
            return carry

        lax.fori_loop(h * count, (h + 1) * count, run, 0)

    def middle(slot, h):
        mine = slice(h * chunks, (h + 1) * chunks)

        def step(p, carry):
            columns = []
            for pair in range(2):
                pieces = []
                for d in range(2):
                    pieces += crossed(
                        state[mine, d, 4 * p + 2 * pair].reshape(chunks * low, lanes),
                        state[mine, d, 4 * p + 2 * pair + 1].reshape(chunks * low, lanes),
                    )
                columns.append(jnp.concatenate(pieces, axis=0))
            result = apply(slot, jnp.concatenate(columns, axis=1))
            for pair in range(2):
                piece = result[:, pair * lanes : (pair + 1) * lanes]
                for d in range(2):
                    start = d * order
                    both = crossed(
                        piece[start : start + chunks * low],
                        piece[start + chunks * low : start + order],
                    )
                    for own in range(2):
                        state[mine, d, 4 * p + 2 * pair + own] = both[own].reshape(
                            chunks, low, lanes
                        )
            return carry

        lax.fori_loop(0, high // 4, step, 0)

    def swap_copy(which, i, bit, device):
        return pltpu.make_async_remote_copy(
            src_ref=state.at[pl.ds(2 * i, 2), :, pl.ds((1 - bit) * half, half)],
            dst_ref=arrived.at[which, pl.ds(2 * i, 2)],
            send_sem=swap_send.at[which, i],
            recv_sem=swap_recv.at[which, i],
            device_id=device,
            device_id_type=MESH,
        )

    def swap_out(slot, h, which, bit, device):
        def send(i):
            top_step(slot, i)
            swap_copy(which, i, bit, device).start()

        each(h, send)

    def swap_in(slot, h, which, bit, device):
        def receive(i):
            swap_copy(which, i, bit, device).wait()
            state[pl.ds(2 * i, 2), :, pl.ds((1 - bit) * half, half)] = arrived[
                which, pl.ds(2 * i, 2)
            ]
            top_step(slot, i)

        each(h, receive)

    def lows(value):
        parts = jnp.concatenate([value[:order], value[order:]], axis=1)
        top, bottom = split(parts)
        joined = jnp.concatenate([top, bottom, top], axis=1)
        result = dot32(joined, low_weight[...])
        return jnp.concatenate([result[:, :lanes], result[:, lanes:]], axis=0)

    def gate(seg, number):
        return gates_ref.at[seg, number]

    set_top(0, gate(0, 0))

    def load(i, carry):
        value = jnp.concatenate(
            [
                amp_ref[pl.ds(2 * i, 2 * order, stride=kk), :],
                amp_ref[pl.ds(2 * i + 1, 2 * order, stride=kk), :],
            ],
            axis=1,
        )
        result = apply(0, value)
        both = crossed(result[:, :lanes], result[:, lanes:])
        for h in range(2):
            state[h * chunks + i] = both[h].reshape(2, high, low, lanes)
        return carry

    lax.fori_loop(0, chunks, load, 0)
    near_bit = r % 2
    set_middle(1, gate(0, 1))
    set_top(2, gate(0, 3))
    middle(1, 0)
    pl.semaphore_wait(barrier, rows)
    swap_out(2, 0, 0, near_bit, (near, c))
    middle(1, 1)
    swap_out(2, 1, 0, near_bit, (near, c))
    set_top(3, gate(1, 0))
    set_middle(4, gate(1, 1))
    set_top(5, gate(1, 3))
    for h in range(2):
        swap_in(3, h, 0, near_bit, (near, c))
        middle(4, h)
        swap_out(5, h, 1, far_bit, (far, c))

    set_top(6, gate(2, 0))
    set_middle(7, gate(2, 1))
    set_top(8, gate(2, 3))
    set_top(9, first_ref)
    for seg in range(3, 5):
        if seg > 3:
            set_top(3 * seg, gate(seg, 0))
        set_middle(3 * seg + 1, gate(seg, 1))
        set_top(3 * seg + 2, gate(seg, 3))
    merged = real_form_transposed(gates_ref[0, 2, 0], gates_ref[0, 2, 1])
    for seg in range(1, gates_ref.shape[0]):
        merged = product(
            merged, real_form_transposed(gates_ref[seg, 2, 0], gates_ref[seg, 2, 1])
        )
    top, bottom = split(merged)
    low_weight[0 : 2 * lanes] = top
    low_weight[2 * lanes : 4 * lanes] = top
    low_weight[4 * lanes : 6 * lanes] = bottom

    def map_copy(i, step):
        target = (r + step) % rows
        return pltpu.make_async_remote_copy(
            src_ref=stage.at[i, target],
            dst_ref=blocks.at[i, r],
            send_sem=map_send.at[i, step],
            recv_sem=map_recv.at[i, step],
            device_id=(target, c),
            device_id_type=MESH,
        )

    def map_out(i):
        result = apply(8, get(i))
        for own in range(2):
            for d in range(2):
                piece = result[
                    d * order : (d + 1) * order, own * lanes : (own + 1) * lanes
                ]
                if rest == 8:
                    stage[i, :, d, own * rest : (own + 1) * rest] = piece.reshape(
                        rows, rest, lanes
                    )
                else:
                    for t in range(rows):
                        stage[i, t, d, own * rest : (own + 1) * rest] = piece[
                            t * rest : (t + 1) * rest
                        ]
        for step in range(1, rows):
            map_copy(i, step).start()
        blocks[i, r] = stage[i, r]

    def map_in(i):
        for step in range(1, rows):
            map_copy(i, step).wait()
        columns = []
        for own in range(2):
            if rest == 8:
                pieces = [
                    blocks[i, :, d, own * rest : (own + 1) * rest].reshape(order, lanes)
                    for d in range(2)
                ]
            else:
                pieces = [
                    blocks[i, s, d, own * rest : (own + 1) * rest]
                    for d in range(2)
                    for s in range(rows)
                ]
            columns.append(jnp.concatenate(pieces, axis=0))
        put(i, apply(9, jnp.concatenate(columns, axis=1)))

    for h in range(2):
        swap_in(6, h, 1, far_bit, (far, c))
        middle(7, h)
        each(h, map_out)
    for h in range(2):
        each(h, map_in)
        middle(10, h)
        swap_out(11, h, 2, col_bit, (r, across))
    for h in range(2):
        swap_in(12, h, 2, col_bit, (r, across))
        middle(13, h)

    def finish(i, carry):
        value = jnp.concatenate(
            [state[h * chunks + i].reshape(2 * order, lanes) for h in range(2)], axis=1
        )
        result = apply(14, value)
        both = crossed(result[:, :lanes], result[:, lanes:])
        for own in range(2):
            out_ref[pl.ds(2 * i + own, 2 * order, stride=kk), :] = lows(both[own])
        return carry

    lax.fori_loop(0, chunks, finish, 0)


def body(amplitudes, gate_matrices, permutation):
    rows = lax.axis_size("row")
    cols = lax.axis_size("col")
    order = gate_matrices.shape[-1]
    amp_count = amplitudes.shape[-1]
    high = amp_count // (order * order)
    low = order // high
    kk = order // low
    rest = order // rows
    chunks = kk // 2
    chosen = (permutation[:, None] == jnp.arange(rows)[None, :]).astype(F32)
    first = jnp.einsum(
        "xjtw,ts->xjsw",
        gate_matrices[3, 0].reshape(2, order, rows, rest),
        chosen,
        precision=HIGHEST,
    ).reshape(2, order, order)
    vmem = pl.BlockSpec(memory_space=pltpu.VMEM)
    result = pl.pallas_call(
        functools.partial(kernel, rows, cols),
        out_shape=jax.ShapeDtypeStruct((2 * amp_count // order, order), F32),
        in_specs=[vmem] * 3,
        out_specs=vmem,
        scratch_shapes=[
            pltpu.VMEM((kk, 2, high, low, order), F32),
            pltpu.VMEM((15, 2 * order, 6 * order), BF16),
            pltpu.VMEM((6 * order, 2 * order), BF16),
            pltpu.VMEM((3, kk, 2, high // 2, low, order), F32),
            pltpu.VMEM((chunks, rows, 2, 2 * rest, order), F32),
            pltpu.VMEM((chunks, rows, 2, 2 * rest, order), F32),
            pltpu.SemaphoreType.DMA((3, chunks)),
            pltpu.SemaphoreType.DMA((3, chunks)),
            pltpu.SemaphoreType.DMA((chunks, rows)),
            pltpu.SemaphoreType.DMA((chunks, rows)),
        ],
        compiler_params=pltpu.CompilerParams(
            collective_id=0, has_side_effects=True, vmem_limit_bytes=48 * 2**20
        ),
    )(amplitudes.reshape(2 * amp_count // order, order), gate_matrices, first)
    return result.reshape(amplitudes.shape)


def solution(mesh):
    placed = (P(None, "row", "col", None), P(), P())
    return jax.shard_map(
        body, mesh=mesh, in_specs=placed, out_specs=P(None, "row", "col", None), check_vma=False
    )
```

```python
import functools

import jax
import jax.numpy as jnp
from jax import lax
from jax.experimental import pallas as pl
from jax.experimental.pallas import tpu as pltpu
from jax.sharding import PartitionSpec as P

MESH = pl.DeviceIdType.MESH
F32 = jnp.float32
BF16 = jnp.bfloat16


def split(value):
    high = value.astype(BF16)
    return high, (value - high.astype(F32)).astype(BF16)


def dot32(left, right):
    return jnp.dot(left, right, preferred_element_type=F32)


def product(left, right):
    left_high, left_low = split(left)
    right_high, right_low = split(right)
    return (
        dot32(left_high, right_high)
        + dot32(left_high, right_low)
        + dot32(left_low, right_high)
    )


def real_form(real_part, imag_part):
    return jnp.concatenate(
        [
            jnp.concatenate([real_part, -imag_part], axis=1),
            jnp.concatenate([imag_part, real_part], axis=1),
        ],
        axis=0,
    )


def real_form_transposed(real_part, imag_part):
    real_t, imag_t = real_part.T, imag_part.T
    return jnp.concatenate(
        [
            jnp.concatenate([real_t, imag_t], axis=1),
            jnp.concatenate([-imag_t, real_t], axis=1),
        ],
        axis=0,
    )


def kernel(
    rows,
    cols,
    amp_ref,
    gates_ref,
    target_ref,
    out_ref,
    state,
    weight,
    low_weight,
    arrived,
    stage,
    blocks,
    swap_send,
    swap_recv,
    map_send,
    map_recv,
):
    kk, _, high, low, lanes = state.shape
    order = high * low
    chunks = kk // 2
    rest = order // rows
    half = high // 2
    r = lax.axis_index("row")
    c = lax.axis_index("col")

    barrier = pltpu.get_barrier_semaphore()
    near = r + 1 - 2 * (r % 2)
    far_bit = r // (rows // 2)
    far = r + rows // 2 - rows * far_bit
    col_bit = c // (cols // 2)
    across = c + cols // 2 - cols * col_bit
    for step in range(1, rows):
        pl.semaphore_signal(
            barrier, inc=1, device_id=((r + step) % rows, c), device_id_type=MESH
        )
    pl.semaphore_signal(barrier, inc=1, device_id=(r, across), device_id_type=MESH)

    count = chunks // 2
    mid_lane = lanes // 2

    def place_weight(slot, top, bottom):
        size = 2 * order
        weight[slot, :, 0:size] = top
        weight[slot, :, size : 2 * size] = top
        weight[slot, :, 2 * size : 3 * size] = bottom

    def set_top(slot, source):
        place_weight(slot, *split(real_form(source[0], source[1])))

    def reorder_matrix():
        new = lax.broadcasted_iota(jnp.int32, (order, order), 0)
        old = lax.broadcasted_iota(jnp.int32, (order, order), 1)
        outer = new // low
        place = (new % low) * kk + 2 * (outer % chunks) + outer // chunks
        return (place == old).astype(F32).astype(BF16)

    def set_middle(slot, source):
        reorder = reorder_matrix()

        def moved(part):
            rows_moved = dot32(reorder, part).astype(BF16)
            return lax.dot_general(
                rows_moved, reorder, (((1,), (1,)), ((), ())), preferred_element_type=F32
            ).astype(BF16)

        real_parts = split(source[0])
        imag_parts = split(source[1])
        place_weight(
            slot,
            *(real_form(moved(re), moved(im)) for re, im in zip(real_parts, imag_parts)),
        )

    def crossed(first, second):
        return (
            jnp.concatenate([first[:, :mid_lane], second[:, :mid_lane]], axis=1),
            jnp.concatenate([first[:, mid_lane:], second[:, mid_lane:]], axis=1),
        )

    def apply(slot, value):
        top, bottom = split(value)
        return dot32(weight[slot], jnp.concatenate([top, bottom, top], axis=0))

    def put(i, result):
        state[2 * i] = result[:, :lanes].reshape(2, high, low, lanes)
        state[2 * i + 1] = result[:, lanes:].reshape(2, high, low, lanes)

    def get(i):
        return jnp.concatenate(
            [
                state[2 * i].reshape(2 * order, lanes),
                state[2 * i + 1].reshape(2 * order, lanes),
            ],
            axis=1,
        )

    def top_step(slot, i):
        put(i, apply(slot, get(i)))

    def each(h, step):
        def run(i, carry):
            step(i)
            return carry

        lax.fori_loop(h * count, (h + 1) * count, run, 0)

    def middle(slot, h):
        mine = slice(h * chunks, (h + 1) * chunks)

        def step(p, carry):
            columns = []
            for pair in range(2):
                pieces = []
                for d in range(2):
                    pieces += crossed(
                        state[mine, d, 4 * p + 2 * pair].reshape(chunks * low, lanes),
                        state[mine, d, 4 * p + 2 * pair + 1].reshape(chunks * low, lanes),
                    )
                columns.append(jnp.concatenate(pieces, axis=0))
            result = apply(slot, jnp.concatenate(columns, axis=1))
            for pair in range(2):
                piece = result[:, pair * lanes : (pair + 1) * lanes]
                for d in range(2):
                    start = d * order
                    both = crossed(
                        piece[start : start + chunks * low],
                        piece[start + chunks * low : start + order],
                    )
                    for own in range(2):
                        state[mine, d, 4 * p + 2 * pair + own] = both[own].reshape(
                            chunks, low, lanes
                        )
            return carry

        lax.fori_loop(0, high // 4, step, 0)

    def swap_copy(which, i, bit, device):
        return pltpu.make_async_remote_copy(
            src_ref=state.at[pl.ds(2 * i, 2), :, pl.ds((1 - bit) * half, half)],
            dst_ref=arrived.at[which, pl.ds(2 * i, 2)],
            send_sem=swap_send.at[which, i],
            recv_sem=swap_recv.at[which, i],
            device_id=device,
            device_id_type=MESH,
        )

    def swap_out(slot, h, which, bit, device):
        def send(i):
            top_step(slot, i)
            swap_copy(which, i, bit, device).start()

        each(h, send)

    def swap_in(slot, h, which, bit, device):
        def receive(i):
            swap_copy(which, i, bit, device).wait()
            state[pl.ds(2 * i, 2), :, pl.ds((1 - bit) * half, half)] = arrived[
                which, pl.ds(2 * i, 2)
            ]
            top_step(slot, i)

        each(h, receive)

    def gate(seg, number):
        return gates_ref.at[seg, number]

    set_top(0, gate(0, 0))

    def load(h):
        def step(i):
            columns = []
            for own in range(2):
                chunk = 2 * (i - h * count) + own
                columns.append(
                    crossed(
                        amp_ref[pl.ds(2 * chunk, 2 * order, stride=kk), :],
                        amp_ref[pl.ds(2 * chunk + 1, 2 * order, stride=kk), :],
                    )[h]
                )
            put(i, apply(0, jnp.concatenate(columns, axis=1)))

        each(h, step)

    near_bit = r % 2
    load(0)
    set_middle(1, gate(0, 1))
    middle(1, 0)
    set_top(2, gate(0, 3))
    pl.semaphore_wait(barrier, rows)
    swap_out(2, 0, 0, near_bit, (near, c))
    set_top(3, gate(1, 0))
    set_middle(4, gate(1, 1))
    set_top(5, gate(1, 3))
    swap_in(3, 0, 0, near_bit, (near, c))
    middle(4, 0)
    swap_out(5, 0, 1, far_bit, (far, c))
    load(1)
    middle(1, 1)
    swap_out(2, 1, 0, near_bit, (near, c))
    swap_in(3, 1, 0, near_bit, (near, c))
    middle(4, 1)
    swap_out(5, 1, 1, far_bit, (far, c))

    set_top(6, gate(2, 0))
    set_middle(7, gate(2, 1))
    set_top(8, gate(2, 3))
    chosen = (
        target_ref[...] == lax.broadcasted_iota(jnp.int32, (order, order), 0)
    ).astype(F32).astype(BF16)

    def turned(part):
        return lax.dot_general(
            part, chosen, (((1,), (1,)), ((), ())), preferred_element_type=F32
        ).astype(BF16)

    parts = zip(split(gates_ref[3, 0, 0]), split(gates_ref[3, 0, 1]))
    place_weight(9, *(real_form(turned(re), turned(im)) for re, im in parts))
    for seg in range(3, 5):
        if seg > 3:
            set_top(3 * seg, gate(seg, 0))
        set_middle(3 * seg + 1, gate(seg, 1))
        set_top(3 * seg + 2, gate(seg, 3))
    merged = real_form_transposed(gates_ref[0, 2, 0], gates_ref[0, 2, 1])
    for seg in range(1, gates_ref.shape[0]):
        merged = product(
            merged, real_form_transposed(gates_ref[seg, 2, 0], gates_ref[seg, 2, 1])
        )
    top, bottom = split(merged)
    for h in range(2):
        for place, part in enumerate((top, top, bottom)):
            low_weight[h, place * lanes : (place + 1) * lanes] = jnp.concatenate(
                [
                    part[h * mid_lane : (h + 1) * mid_lane],
                    part[lanes + h * mid_lane : lanes + (h + 1) * mid_lane],
                ],
                axis=0,
            )

    def map_copy(i, step):
        target = (r + step) % rows
        return pltpu.make_async_remote_copy(
            src_ref=stage.at[i, target],
            dst_ref=blocks.at[i, r],
            send_sem=map_send.at[i, step],
            recv_sem=map_recv.at[i, step],
            device_id=(target, c),
            device_id_type=MESH,
        )

    def map_out(i):
        result = apply(8, get(i))
        for own in range(2):
            for d in range(2):
                piece = result[
                    d * order : (d + 1) * order, own * lanes : (own + 1) * lanes
                ]
                if rest == 8:
                    stage[i, :, d, own * rest : (own + 1) * rest] = piece.reshape(
                        rows, rest, lanes
                    )
                else:
                    for t in range(rows):
                        stage[i, t, d, own * rest : (own + 1) * rest] = piece[
                            t * rest : (t + 1) * rest
                        ]
        for step in range(1, rows):
            map_copy(i, step).start()
        blocks[i, r] = stage[i, r]

    def map_in(i):
        for step in range(1, rows):
            map_copy(i, step).wait()
        columns = []
        for own in range(2):
            if rest == 8:
                pieces = [
                    blocks[i, :, d, own * rest : (own + 1) * rest].reshape(order, lanes)
                    for d in range(2)
                ]
            else:
                pieces = [
                    blocks[i, s, d, own * rest : (own + 1) * rest]
                    for d in range(2)
                    for s in range(rows)
                ]
            columns.append(jnp.concatenate(pieces, axis=0))
        put(i, apply(9, jnp.concatenate(columns, axis=1)))

    for h in range(2):
        swap_in(6, h, 1, far_bit, (far, c))
        middle(7, h)
        each(h, map_out)
    for h in range(2):
        each(h, map_in)
        middle(10, h)
        swap_out(11, h, 2, col_bit, (r, across))
    def finish(h):
        def step(i):
            result = apply(14, get(i))
            for own in range(2):
                piece = result[:, own * lanes : (own + 1) * lanes]
                both = crossed(piece[:order], piece[order:])
                for odd in range(2):
                    top, bottom = split(both[odd])
                    share = dot32(
                        jnp.concatenate([top, bottom, top], axis=1), low_weight[h]
                    )
                    k = 2 * (2 * (i - h * count) + own) + odd
                    for d in range(2):
                        where = pl.ds(d * order * kk + k, order, stride=kk)
                        value = share[:, d * lanes : (d + 1) * lanes]
                        if h:
                            value = value + out_ref[where, :]
                        out_ref[where, :] = value

        each(h, step)

    for h in range(2):
        swap_in(12, h, 2, col_bit, (r, across))
        middle(13, h)
        finish(h)


def body(amplitudes, gate_matrices, permutation):
    rows = lax.axis_size("row")
    cols = lax.axis_size("col")
    order = gate_matrices.shape[-1]
    amp_count = amplitudes.shape[-1]
    high = amp_count // (order * order)
    low = order // high
    kk = order // low
    rest = order // rows
    chunks = kk // 2
    target = permutation[:, None] * rest + jnp.arange(rest, dtype=jnp.int32)[None, :]
    target = target.reshape(1, order)
    vmem = pl.BlockSpec(memory_space=pltpu.VMEM)
    result = pl.pallas_call(
        functools.partial(kernel, rows, cols),
        out_shape=jax.ShapeDtypeStruct((2 * amp_count // order, order), F32),
        in_specs=[vmem] * 3,
        out_specs=vmem,
        scratch_shapes=[
            pltpu.VMEM((kk, 2, high, low, order), F32),
            pltpu.VMEM((15, 2 * order, 6 * order), BF16),
            pltpu.VMEM((2, 3 * order, 2 * order), BF16),
            pltpu.VMEM((3, kk, 2, high // 2, low, order), F32),
            pltpu.VMEM((chunks, rows, 2, 2 * rest, order), F32),
            pltpu.VMEM((chunks, rows, 2, 2 * rest, order), F32),
            pltpu.SemaphoreType.DMA((3, chunks)),
            pltpu.SemaphoreType.DMA((3, chunks)),
            pltpu.SemaphoreType.DMA((chunks, rows)),
            pltpu.SemaphoreType.DMA((chunks, rows)),
        ],
        compiler_params=pltpu.CompilerParams(
            collective_id=0, has_side_effects=True, vmem_limit_bytes=48 * 2**20
        ),
    )(amplitudes.reshape(2 * amp_count // order, order), gate_matrices, target)
    return result.reshape(amplitudes.shape)


def solution(mesh):
    placed = (P(None, "row", "col", None), P(), P())
    return jax.shard_map(
        body, mesh=mesh, in_specs=placed, out_specs=P(None, "row", "col", None), check_vma=False
    )
```

```python
import functools

import jax
import jax.numpy as jnp
from jax import lax
from jax.experimental import pallas as pl
from jax.experimental.pallas import tpu as pltpu
from jax.sharding import PartitionSpec as P

MESH = pl.DeviceIdType.MESH
F32 = jnp.float32
BF16 = jnp.bfloat16


def split(value):
    high = value.astype(BF16)
    return high, (value - high.astype(F32)).astype(BF16)


def dot32(left, right):
    return jnp.dot(left, right, preferred_element_type=F32)


def product(left, right):
    left_high, left_low = split(left)
    right_high, right_low = split(right)
    return (
        dot32(left_high, right_high)
        + dot32(left_high, right_low)
        + dot32(left_low, right_high)
    )


def real_form(real_part, imag_part):
    return jnp.concatenate(
        [
            jnp.concatenate([real_part, -imag_part], axis=1),
            jnp.concatenate([imag_part, real_part], axis=1),
        ],
        axis=0,
    )


def real_form_transposed(real_part, imag_part):
    real_t, imag_t = real_part.T, imag_part.T
    return jnp.concatenate(
        [
            jnp.concatenate([real_t, imag_t], axis=1),
            jnp.concatenate([-imag_t, real_t], axis=1),
        ],
        axis=0,
    )


def kernel(
    rows,
    cols,
    amp_ref,
    gates_ref,
    target_ref,
    out_ref,
    state,
    weight,
    low_weight,
    arrived,
    stage,
    blocks,
    swap_send,
    swap_recv,
    map_send,
    map_recv,
):
    kk, _, high, low, lanes = state.shape
    order = high * low
    chunks = kk // 2
    rest = order // rows
    half = high // 2
    r = lax.axis_index("row")
    c = lax.axis_index("col")

    barrier = pltpu.get_barrier_semaphore()
    near = r + 1 - 2 * (r % 2)
    far_bit = r // (rows // 2)
    far = r + rows // 2 - rows * far_bit
    col_bit = c // (cols // 2)
    across = c + cols // 2 - cols * col_bit
    for step in range(1, rows):
        pl.semaphore_signal(
            barrier, inc=1, device_id=((r + step) % rows, c), device_id_type=MESH
        )
    pl.semaphore_signal(barrier, inc=1, device_id=(r, across), device_id_type=MESH)

    count = chunks // 2
    mid_lane = lanes // 2

    def place_weight(slot, top, bottom):
        size = 2 * order
        weight[slot, :, 0:size] = top
        weight[slot, :, size : 2 * size] = top
        weight[slot, :, 2 * size : 3 * size] = bottom

    def set_top(slot, source):
        place_weight(slot, *split(real_form(source[0], source[1])))

    def reorder_matrix():
        new = lax.broadcasted_iota(jnp.int32, (order, order), 0)
        old = lax.broadcasted_iota(jnp.int32, (order, order), 1)
        outer = new // low
        place = (new % low) * kk + 2 * (outer % chunks) + outer // chunks
        return (place == old).astype(F32).astype(BF16)

    def set_middle(slot, source):
        reorder = reorder_matrix()

        def moved(part):
            rows_moved = dot32(reorder, part).astype(BF16)
            return lax.dot_general(
                rows_moved, reorder, (((1,), (1,)), ((), ())), preferred_element_type=F32
            ).astype(BF16)

        real_parts = split(source[0])
        imag_parts = split(source[1])
        place_weight(
            slot,
            *(real_form(moved(re), moved(im)) for re, im in zip(real_parts, imag_parts)),
        )

    def crossed(first, second):
        return (
            jnp.concatenate([first[:, :mid_lane], second[:, :mid_lane]], axis=1),
            jnp.concatenate([first[:, mid_lane:], second[:, mid_lane:]], axis=1),
        )

    def apply(slot, value):
        top, bottom = split(value)
        return dot32(weight[slot], jnp.concatenate([top, bottom, top], axis=0))

    def put(i, result):
        state[2 * i] = result[:, :lanes].reshape(2, high, low, lanes)
        state[2 * i + 1] = result[:, lanes:].reshape(2, high, low, lanes)

    def get(i):
        return jnp.concatenate(
            [
                state[2 * i].reshape(2 * order, lanes),
                state[2 * i + 1].reshape(2 * order, lanes),
            ],
            axis=1,
        )

    def top_step(slot, i):
        put(i, apply(slot, get(i)))

    def each(h, step, unroll=4):
        def run(i, carry):
            step(i)
            return carry

        lax.fori_loop(h * count, (h + 1) * count, run, 0, unroll=unroll)

    def middle(slot, h):
        mine = slice(h * chunks, (h + 1) * chunks)

        def step(p, carry):
            columns = []
            for pair in range(2):
                pieces = []
                for d in range(2):
                    pieces += crossed(
                        state[mine, d, 4 * p + 2 * pair].reshape(chunks * low, lanes),
                        state[mine, d, 4 * p + 2 * pair + 1].reshape(chunks * low, lanes),
                    )
                columns.append(jnp.concatenate(pieces, axis=0))
            result = apply(slot, jnp.concatenate(columns, axis=1))
            for pair in range(2):
                piece = result[:, pair * lanes : (pair + 1) * lanes]
                for d in range(2):
                    start = d * order
                    both = crossed(
                        piece[start : start + chunks * low],
                        piece[start + chunks * low : start + order],
                    )
                    for own in range(2):
                        state[mine, d, 4 * p + 2 * pair + own] = both[own].reshape(
                            chunks, low, lanes
                        )
            return carry

        lax.fori_loop(0, high // 4, step, 0, unroll=4)

    def swap_copy(which, i, bit, device):
        return pltpu.make_async_remote_copy(
            src_ref=state.at[pl.ds(2 * i, 2), :, pl.ds((1 - bit) * half, half)],
            dst_ref=arrived.at[which, pl.ds(2 * i, 2)],
            send_sem=swap_send.at[which, i],
            recv_sem=swap_recv.at[which, i],
            device_id=device,
            device_id_type=MESH,
        )

    def swap_out(slot, h, which, bit, device):
        def send(i):
            top_step(slot, i)
            swap_copy(which, i, bit, device).start()

        each(h, send)

    def swap_in(slot, h, which, bit, device):
        def receive(i):
            swap_copy(which, i, bit, device).wait()
            state[pl.ds(2 * i, 2), :, pl.ds((1 - bit) * half, half)] = arrived[
                which, pl.ds(2 * i, 2)
            ]
            top_step(slot, i)

        each(h, receive)

    def gate(seg, number):
        return gates_ref.at[seg, number]

    set_top(0, gate(0, 0))

    def load(h):
        def step(i):
            columns = []
            for own in range(2):
                chunk = 2 * (i - h * count) + own
                columns.append(
                    crossed(
                        amp_ref[pl.ds(2 * chunk, 2 * order, stride=kk), :],
                        amp_ref[pl.ds(2 * chunk + 1, 2 * order, stride=kk), :],
                    )[h]
                )
            put(i, apply(0, jnp.concatenate(columns, axis=1)))

        each(h, step)

    near_bit = r % 2
    load(0)
    set_middle(1, gate(0, 1))
    middle(1, 0)
    set_top(2, gate(0, 3))
    pl.semaphore_wait(barrier, rows)
    swap_out(2, 0, 0, near_bit, (near, c))
    set_top(3, gate(1, 0))
    set_middle(4, gate(1, 1))
    set_top(5, gate(1, 3))
    swap_in(3, 0, 0, near_bit, (near, c))
    middle(4, 0)
    swap_out(5, 0, 1, far_bit, (far, c))
    load(1)
    middle(1, 1)
    swap_out(2, 1, 0, near_bit, (near, c))
    swap_in(3, 1, 0, near_bit, (near, c))
    middle(4, 1)
    swap_out(5, 1, 1, far_bit, (far, c))

    set_top(6, gate(2, 0))
    set_middle(7, gate(2, 1))
    set_top(8, gate(2, 3))
    chosen = (
        target_ref[...] == lax.broadcasted_iota(jnp.int32, (order, order), 0)
    ).astype(F32).astype(BF16)

    def turned(part):
        return lax.dot_general(
            part, chosen, (((1,), (1,)), ((), ())), preferred_element_type=F32
        ).astype(BF16)

    parts = zip(split(gates_ref[3, 0, 0]), split(gates_ref[3, 0, 1]))
    place_weight(9, *(real_form(turned(re), turned(im)) for re, im in parts))
    for seg in range(3, 5):
        if seg > 3:
            set_top(3 * seg, gate(seg, 0))
        set_middle(3 * seg + 1, gate(seg, 1))
        set_top(3 * seg + 2, gate(seg, 3))
    merged = real_form_transposed(gates_ref[0, 2, 0], gates_ref[0, 2, 1])
    for seg in range(1, gates_ref.shape[0]):
        merged = product(
            merged, real_form_transposed(gates_ref[seg, 2, 0], gates_ref[seg, 2, 1])
        )
    top, bottom = split(merged)
    for h in range(2):
        for place, part in enumerate((top, top, bottom)):
            low_weight[h, place * lanes : (place + 1) * lanes] = jnp.concatenate(
                [
                    part[h * mid_lane : (h + 1) * mid_lane],
                    part[lanes + h * mid_lane : lanes + (h + 1) * mid_lane],
                ],
                axis=0,
            )

    def map_copy(i, step):
        target = (r + step) % rows
        return pltpu.make_async_remote_copy(
            src_ref=stage.at[i, target],
            dst_ref=blocks.at[i, r],
            send_sem=map_send.at[i, step],
            recv_sem=map_recv.at[i, step],
            device_id=(target, c),
            device_id_type=MESH,
        )

    def map_out(i):
        result = apply(8, get(i))
        for own in range(2):
            for d in range(2):
                piece = result[
                    d * order : (d + 1) * order, own * lanes : (own + 1) * lanes
                ]
                if rest == 8:
                    stage[i, :, d, own * rest : (own + 1) * rest] = piece.reshape(
                        rows, rest, lanes
                    )
                else:
                    for t in range(rows):
                        stage[i, t, d, own * rest : (own + 1) * rest] = piece[
                            t * rest : (t + 1) * rest
                        ]
        for step in range(1, rows):
            map_copy(i, step).start()
        blocks[i, r] = stage[i, r]

    def map_in(i):
        for step in range(1, rows):
            map_copy(i, step).wait()
        columns = []
        for own in range(2):
            if rest == 8:
                pieces = [
                    blocks[i, :, d, own * rest : (own + 1) * rest].reshape(order, lanes)
                    for d in range(2)
                ]
            else:
                pieces = [
                    blocks[i, s, d, own * rest : (own + 1) * rest]
                    for d in range(2)
                    for s in range(rows)
                ]
            columns.append(jnp.concatenate(pieces, axis=0))
        put(i, apply(9, jnp.concatenate(columns, axis=1)))

    for h in range(2):
        swap_in(6, h, 1, far_bit, (far, c))
        middle(7, h)
        each(h, map_out, 1)
    for h in range(2):
        each(h, map_in, 1)
        middle(10, h)
        swap_out(11, h, 2, col_bit, (r, across))
    def finish(h):
        def step(i):
            result = apply(14, get(i))
            for own in range(2):
                piece = result[:, own * lanes : (own + 1) * lanes]
                both = crossed(piece[:order], piece[order:])
                for odd in range(2):
                    top, bottom = split(both[odd])
                    share = dot32(
                        jnp.concatenate([top, bottom, top], axis=1), low_weight[h]
                    )
                    k = 2 * (2 * (i - h * count) + own) + odd
                    for d in range(2):
                        where = pl.ds(d * order * kk + k, order, stride=kk)
                        value = share[:, d * lanes : (d + 1) * lanes]
                        if h:
                            value = value + out_ref[where, :]
                        out_ref[where, :] = value

        each(h, step)

    for h in range(2):
        swap_in(12, h, 2, col_bit, (r, across))
        middle(13, h)
        finish(h)


def body(amplitudes, gate_matrices, permutation):
    rows = lax.axis_size("row")
    cols = lax.axis_size("col")
    order = gate_matrices.shape[-1]
    amp_count = amplitudes.shape[-1]
    high = amp_count // (order * order)
    low = order // high
    kk = order // low
    rest = order // rows
    chunks = kk // 2
    target = permutation[:, None] * rest + jnp.arange(rest, dtype=jnp.int32)[None, :]
    target = target.reshape(1, order)
    vmem = pl.BlockSpec(memory_space=pltpu.VMEM)
    result = pl.pallas_call(
        functools.partial(kernel, rows, cols),
        out_shape=jax.ShapeDtypeStruct((2 * amp_count // order, order), F32),
        in_specs=[vmem] * 3,
        out_specs=vmem,
        scratch_shapes=[
            pltpu.VMEM((kk, 2, high, low, order), F32),
            pltpu.VMEM((15, 2 * order, 6 * order), BF16),
            pltpu.VMEM((2, 3 * order, 2 * order), BF16),
            pltpu.VMEM((3, kk, 2, high // 2, low, order), F32),
            pltpu.VMEM((chunks, rows, 2, 2 * rest, order), F32),
            pltpu.VMEM((chunks, rows, 2, 2 * rest, order), F32),
            pltpu.SemaphoreType.DMA((3, chunks)),
            pltpu.SemaphoreType.DMA((3, chunks)),
            pltpu.SemaphoreType.DMA((chunks, rows)),
            pltpu.SemaphoreType.DMA((chunks, rows)),
        ],
        compiler_params=pltpu.CompilerParams(
            collective_id=0, has_side_effects=True, vmem_limit_bytes=48 * 2**20
        ),
    )(amplitudes.reshape(2 * amp_count // order, order), gate_matrices, target)
    return result.reshape(amplitudes.shape)


def solution(mesh):
    placed = (P(None, "row", "col", None), P(), P())
    return jax.shard_map(
        body, mesh=mesh, in_specs=placed, out_specs=P(None, "row", "col", None), check_vma=False
    )
```
